32 devices in a mesh: ctx: 4 (over y, x), tp: 8 (over z, core).
Axes of the slice: x: 2, y: 2, z: 4, core: 2. Of those that a mesh axis runs over, the one named last changes fastest.
Arguments:
- queries: bfloat16 [896, 8192], P('ctx', 'tp'), may hold values from -8 to 8
- keys: bfloat16 [896, 1024], P('ctx'), may hold values from -8 to 8
- values: bfloat16 [896, 1024], P('ctx'), may hold values from -32 to 32
- out_weight: bfloat16 [8192, 8192], P('tp'), may hold values from -0.09375 to 0.09375
- signs: int32 [8192], replicated, may hold values from 0 to 1
Outputs:
- rotated_payload: bfloat16 [896, 8192], P('ctx')
- block_scales: float32 [896, 64], P('ctx')
The draws below stay inside these ranges and needn't reach their ends.
All inputs are finite; a program needn't handle non-finite values. Where the reference program divides by a largest or mean magnitude, that divisor is 1e-20 or more.
Results may differ from the reference program's by a relative error of at most 0.0095.
Values may be sent and summed in bfloat16 or wider, within the bound.
A program may use at most 128 MiB of HBM per device.

```python
import math
import jax
import jax.numpy as jnp
from jax import lax

D = 8192
QUERY_HEADS = 64
KEY_VALUE_HEADS = 8
HEAD_SIZE = 128
BLOCK = 128
SEQUENCE_TOKENS = 896
N_TP = 8


def draw_queries(key, part):
    sampled_values = jnp.clip(jax.random.normal(jax.random.fold_in(key, 1), (SEQUENCE_TOKENS, QUERY_HEADS * HEAD_SIZE), jnp.float32), -6.0, 6.0)
    return sampled_values.astype(jnp.bfloat16)


def draw_keys(key, part):
    sampled_values = jnp.clip(jax.random.normal(jax.random.fold_in(key, 2), (SEQUENCE_TOKENS, KEY_VALUE_HEADS * HEAD_SIZE), jnp.float32), -6.0, 6.0)
    return sampled_values.astype(jnp.bfloat16)


def draw_values(key, part):
    sampled_values = jnp.clip(jax.random.normal(jax.random.fold_in(key, 3), (SEQUENCE_TOKENS, KEY_VALUE_HEADS * HEAD_SIZE), jnp.float32), -4.0, 4.0)
    return sampled_values.astype(jnp.bfloat16)


def plant(entries, key, least, largest):
    shape = entries.shape
    index_at = [jax.random.randint(jax.random.fold_in(key, axis), (), 0, shape[axis]) for axis in range(len(shape))]
    entries = entries.at[tuple(index_at)].set(least)
    longest = shape.index(max(shape))
    index_at[longest] = (index_at[longest] + 1) % shape[longest]
    return entries.at[tuple(index_at)].set(largest)


def spiked(values, own_key, source, target, shards_of, factor):
    owner, partner = [(jnp.arange(values.shape[position]) // (values.shape[position] // shards_of)).reshape([-1 if axis == position else 1 for axis in range(values.ndim)]) for position in (source, target)]
    chosen = jax.random.permutation(own_key, shards_of)[partner]
    strong = (owner == chosen) | (owner == (partner + shards_of // 2) % shards_of)
    return jnp.where(strong, factor * values, values)


def steps_of(stream_key, extent, split, low, largest):
    level, own = 1.0, jax.random.fold_in(stream_key, 6)
    for dim, shards_of in split:
        draws = jnp.exp(jax.random.uniform(jax.random.fold_in(own, dim), (shards_of,), jnp.float32, low / len(split), largest / len(split)))
        level = level * jnp.repeat(draws, extent[dim] // shards_of).reshape([-1 if axis == dim else 1 for axis in range(len(extent))])
    return level


def noise_with(key, shape, deviation, reach, cuts, heavy, kind=jnp.bfloat16):
    result = deviation * jax.random.normal(key, shape, jnp.float32)
    if cuts:
        result = result * steps_of(key, shape, cuts, -0.22, 0.18)
    return jnp.clip(spiked(result, jax.random.fold_in(key, 3), *heavy), -reach, reach).astype(kind)


def setup_inputs(seed: int = 0) -> dict:
    key_list = jax.random.split(jax.random.key(seed), 6)
    queries = draw_queries(jax.random.fold_in(key_list[5], 71), 0)
    keys = draw_keys(jax.random.fold_in(key_list[5], 71), 0)
    values = draw_values(jax.random.fold_in(key_list[5], 71), 0)
    out_weight = noise_with(key_list[3], (QUERY_HEADS * HEAD_SIZE, D), (QUERY_HEADS * HEAD_SIZE) ** -0.5, 0.09375, ((0, 8),), (0, 1, 8, 2.0))
    signs = plant(jax.random.randint(key_list[4], (D,), 0, 2), jax.random.fold_in(key_list[4], 1), 0, 1).astype(jnp.int32)
    return dict(queries=queries, keys=keys, values=values, out_weight=out_weight, signs=signs)


clip_ratio = 2.0

def hadamard():
    indices = jnp.arange(BLOCK, dtype=jnp.int32)
    common = jnp.bitwise_and(indices[:, None], indices[None, :])
    parity = jnp.zeros((BLOCK, BLOCK), jnp.int32)
    for bit_index in range(BLOCK.bit_length() - 1):
        parity = parity + jnp.bitwise_and(jnp.right_shift(common, bit_index), 1)
    signed = (1 - 2 * (parity % 2)).astype(jnp.float32)
    return signed * jnp.float32(1.0 / math.sqrt(BLOCK))

def rotate(partial_value, sign_row):
    row_count = partial_value.shape[0]
    flat = (partial_value * sign_row[None, :]).reshape(-1, BLOCK)
    turned = jnp.dot(flat, hadamard(), precision=lax.Precision.HIGHEST)
    return turned.reshape(row_count, D)

def clip_quantize(rotated):
    row_count = rotated.shape[0]
    blocked = rotated.reshape(row_count, -1, BLOCK)
    scales = clip_ratio * jnp.sqrt(lax.optimization_barrier(jnp.mean(blocked * blocked, axis=-1)) + 1e-06)
    payload = jnp.clip(blocked / scales[..., None], -1.0, 1.0).astype(jnp.bfloat16).reshape(row_count, -1)
    return (payload, scales)

def quantize(rotated):
    row_count = rotated.shape[0]
    blocked = rotated.reshape(row_count, -1, BLOCK)
    scales = lax.optimization_barrier(jnp.max(jnp.abs(blocked), axis=-1)) + 1e-06
    payload = (blocked / scales[..., None]).astype(jnp.bfloat16).reshape(row_count, -1)
    return (payload, scales)

def reference(queries, keys, values, out_weight, signs):
    score_scale = 1.0 / math.sqrt(HEAD_SIZE)
    group_width = QUERY_HEADS // KEY_VALUE_HEADS
    positions = jnp.arange(SEQUENCE_TOKENS, dtype=jnp.int32)
    allowed = positions[None, :] <= positions[:, None]
    query_heads = queries.reshape(SEQUENCE_TOKENS, QUERY_HEADS, HEAD_SIZE)
    key_head_count = keys.reshape(SEQUENCE_TOKENS, KEY_VALUE_HEADS, HEAD_SIZE)
    value_head_count = values.reshape(SEQUENCE_TOKENS, KEY_VALUE_HEADS, HEAD_SIZE)

    def one_head(head_index):
        kv_index = head_index // group_width
        query_one = lax.dynamic_index_in_dim(query_heads, head_index, 1, keepdims=False)
        key_one = lax.dynamic_index_in_dim(key_head_count, kv_index, 1, keepdims=False)
        value_one = lax.dynamic_index_in_dim(value_head_count, kv_index, 1, keepdims=False)
        scores = jnp.dot(query_one, key_one.T, preferred_element_type=jnp.float32) * score_scale
        scores = jnp.where(allowed, scores, -1e+30)
        row_max = lax.optimization_barrier(jnp.max(scores, axis=-1, keepdims=True))
        weights = jnp.where(allowed, jnp.exp(scores - row_max), 0.0)
        row_sum = lax.optimization_barrier(jnp.sum(weights, axis=-1, keepdims=True))
        mixed = jnp.dot(weights, value_one.astype(jnp.float32), precision=lax.Precision.HIGHEST)
        return (mixed / row_sum).astype(jnp.bfloat16)
    stacked = lax.map(one_head, jnp.arange(QUERY_HEADS, dtype=jnp.int32))
    attended = jnp.transpose(stacked, (1, 0, 2)).reshape(SEQUENCE_TOKENS, QUERY_HEADS * HEAD_SIZE)
    sign_row = (2 * signs - 1).astype(jnp.float32)
    group_cols = QUERY_HEADS * HEAD_SIZE // N_TP

    def add_group(tp_index, summed):
        start_col = (tp_index * group_cols).astype(jnp.int32)
        attended_part = lax.dynamic_slice_in_dim(attended, start_col, group_cols, 1)
        weight_part = lax.dynamic_slice_in_dim(out_weight, start_col, group_cols, 0)
        partial_value = jnp.dot(attended_part, weight_part, preferred_element_type=jnp.float32)
        payload, scales = clip_quantize(rotate(partial_value, sign_row))
        restored = payload.astype(jnp.float32).reshape(SEQUENCE_TOKENS, -1, BLOCK) * scales[..., None]
        return summed + restored.reshape(SEQUENCE_TOKENS, D)
    summed = lax.fori_loop(0, N_TP, add_group, jnp.zeros((SEQUENCE_TOKENS, D), jnp.float32))
    rotated_payload, block_scales = quantize(summed)
    return (rotated_payload, block_scales)
```

```python
import functools
import math

import jax
import jax.numpy as jnp
from jax import lax
from jax.experimental import pallas as pl
from jax.experimental.pallas import tpu as pltpu
from jax.sharding import PartitionSpec as P

HEAD = 128
BLOCK = 128
CORES = 2
CHUNK = CORES * BLOCK
MID_SKEW = 2
HOP_SKEW = 7
MESH = pl.DeviceIdType.MESH
F32 = jnp.float32
BF16 = jnp.bfloat16


def kernel(
    n_ctx,
    n_tp,
    kv_group,
    q_hbm,
    k_hbm,
    v_hbm,
    w_hbm,
    sign_hbm,
    out_hbm,
    scale_hbm,
    q_ref,
    sign_ref,
    k_all,
    v_all,
    w_all,
    att,
    run_max,
    run_sum,
    run_acc,
    turn_ref,
    ones_ref,
    own,
    sib_out,
    sib_in,
    outer_in,
    mine,
    cross_in,
    total,
    sib_total,
    fin,
    scales,
    load_sem,
    w_sem,
    kv_send,
    kv_recv,
    sib_send,
    sib_recv,
    inward_send,
    outer_recv,
    cross_recv,
    outward_send,
    total_recv,
    share_send,
    share_recv,
    out_sem,
):
    rows, depth = q_ref.shape
    heads = depth // HEAD
    steps = w_all.shape[0]
    ctx = lax.axis_index("ctx")
    tp = lax.axis_index("tp")
    core = lax.rem(tp, CORES)
    chip = tp // CORES
    chips = n_tp // CORES
    half = chips // 2
    left = chip < half
    edge = jnp.where(left, chip, chips - 1 - chip)
    centre = edge == half - 1
    has_outer = edge > 0
    ahead = jnp.where(left, CORES, -CORES)
    sibling = tp + 1 - 2 * core
    inward = tp + ahead
    outward = tp - ahead

    head_at = tp * heads // kv_group
    cols = pl.ds(pl.multiple_of(head_at * HEAD, HEAD), HEAD)

    loads = [
        pltpu.make_async_copy(k_hbm.at[:, cols], k_all.at[ctx], load_sem.at[0]),
        pltpu.make_async_copy(q_hbm, q_ref, load_sem.at[1]),
        pltpu.make_async_copy(v_hbm.at[:, cols], v_all.at[ctx], load_sem.at[2]),
        pltpu.make_async_copy(sign_hbm, sign_ref, load_sem.at[3]),
    ]
    for load in loads:
        load.start()

    barrier = pltpu.get_barrier_semaphore()

    @pl.loop(1, n_ctx)
    def _(step):
        pl.semaphore_signal(
            barrier, inc=1, device_id=(lax.rem(ctx + step, n_ctx), tp), device_id_type=MESH
        )

    pl.semaphore_signal(barrier, inc=1, device_id=(ctx, sibling), device_id_type=MESH)
    pl.semaphore_signal(barrier, inc=1, device_id=(ctx, inward), device_id_type=MESH)

    @pl.when(has_outer)
    def _():
        pl.semaphore_signal(barrier, inc=1, device_id=(ctx, outward), device_id_type=MESH)

    pl.semaphore_wait(barrier, n_ctx + 1 + jnp.where(has_outer, 1, 0))

    def kv_copies(source, target):
        return [
            pltpu.make_async_remote_copy(
                src_ref=hbm.at[:, cols],
                dst_ref=gathered.at[source],
                send_sem=kv_send.at[which, target],
                recv_sem=kv_recv.at[which, source],
                device_id=(target, tp),
                device_id_type=MESH,
            )
            for which, (hbm, gathered) in enumerate(((k_hbm, k_all), (v_hbm, v_all)))
        ]

    @pl.loop(0, n_ctx - 1 - ctx)
    def _(step):
        for copy in kv_copies(ctx, n_ctx - 1 - step):
            copy.start()

    def w_copy(step):
        wide = pl.ds(pl.multiple_of(step * CHUNK, CHUNK), CHUNK)
        return pltpu.make_async_copy(w_hbm.at[:, wide], w_all.at[step], w_sem.at[step])

    @pl.loop(0, steps)
    def _(step):
        w_copy(step).start()

    row_id = lax.broadcasted_iota(jnp.int32, (CHUNK, CHUNK), 0)
    col_id = lax.broadcasted_iota(jnp.int32, (CHUNK, CHUNK), 1)
    same = (row_id // BLOCK) == (col_id // BLOCK)
    common = jnp.bitwise_and(jnp.bitwise_and(row_id, col_id), BLOCK - 1)
    parity = jnp.zeros((CHUNK, CHUNK), jnp.int32)
    for bit in range(BLOCK.bit_length() - 1):
        parity = jnp.bitwise_xor(parity, jnp.right_shift(common, bit))
    odd = jnp.bitwise_and(parity, 1)
    turn_ref[...] = jnp.where(same, (1 - 2 * odd).astype(F32), 0.0).astype(BF16)
    ones_ref[...] = jnp.where(same, 1.0, 0.0).astype(BF16)
    scales[...] = jnp.zeros_like(scales)

    for load in loads:
        load.wait()

    exponent = math.log2(math.e) / math.sqrt(HEAD)

    def absorb(source, diagonal):
        key = k_all[source]
        value_t = v_all[source].astype(F32).T.astype(BF16)
        for h in range(heads):
            query = q_ref[:, h * HEAD : (h + 1) * HEAD]
            scores = lax.dot_general(
                key, query, (((1,), (1,)), ((), ())), preferred_element_type=F32
            )
            scores = scores * exponent
            if diagonal:
                key_pos = lax.broadcasted_iota(jnp.int32, (rows, rows), 0)
                query_pos = lax.broadcasted_iota(jnp.int32, (rows, rows), 1)
                scores = jnp.where(key_pos <= query_pos, scores, -1e30)
            top = jnp.max(scores, axis=0, keepdims=True)
            if not diagonal:
                before = run_max[h]
                top = jnp.maximum(before, top)
                keep = jnp.exp2(before - top)
            weights = jnp.exp2(scores - top)
            weight_sum = jnp.sum(weights, axis=0, keepdims=True)
            mixed = jnp.dot(value_t, weights.astype(BF16), preferred_element_type=F32)
            if not diagonal:
                weight_sum = weight_sum + keep * run_sum[h]
                mixed = mixed + keep * run_acc[h]
            run_max[h] = top
            run_sum[h] = weight_sum
            run_acc[h] = mixed

    absorb(ctx, True)

    @pl.loop(1, ctx + 1)
    def _(back):
        source = ctx - back
        for copy in kv_copies(source, ctx):
            copy.wait_recv()
        absorb(source, False)

    for h in range(heads):
        normed = run_acc[h] / run_sum[h]
        att[:, h * HEAD : (h + 1) * HEAD] = normed.T.astype(BF16)

    def remote(src, dst, send, recv, target):
        return pltpu.make_async_remote_copy(
            src_ref=src,
            dst_ref=dst,
            send_sem=send,
            recv_sem=recv,
            device_id=(ctx, target),
            device_id_type=MESH,
        )

    def sib_copy(k):
        return remote(sib_out.at[k], sib_in.at[k], sib_send.at[k], sib_recv.at[k], sibling)

    def outer_copy(k):
        return remote(mine.at[k], outer_in.at[k], inward_send.at[k], outer_recv.at[k], inward)

    def cross_copy(k):
        return remote(mine.at[k], cross_in.at[k], inward_send.at[k], cross_recv.at[k], inward)

    def total_copy(k):
        return remote(total.at[k], total.at[k], outward_send.at[k], total_recv.at[k], outward)

    def share_copy(k):
        return remote(total.at[k], sib_total.at[k], share_send.at[k], share_recv.at[k], sibling)

    def out_copy(k):
        wide = pl.ds(pl.multiple_of(k * CHUNK, CHUNK), CHUNK)
        return pltpu.make_async_copy(fin.at[k], out_hbm.at[:, wide], out_sem.at[k])

    def project(k):
        w_copy(k).wait()
        part = jnp.dot(att[...], w_all[k], preferred_element_type=F32)
        sign_row = jnp.concatenate(
            [sign_ref[pl.ds(k * CORES + i, 1), :] for i in range(CORES)], axis=1
        )
        part = part * (2 * sign_row - 1).astype(F32)
        turned = jnp.dot(part.astype(BF16), turn_ref[...], preferred_element_type=F32)
        turned = turned * F32(1.0 / math.sqrt(BLOCK))
        squares = jnp.dot((part * part).astype(BF16), ones_ref[...], preferred_element_type=F32)
        limit = 2.0 * jnp.sqrt(squares * F32(1.0 / BLOCK) + 1e-06)
        clipped = jnp.clip(turned, -limit, limit)
        low, high = clipped[:, :BLOCK], clipped[:, BLOCK:]
        sib_out[k] = jnp.where(core == 0, high, low).astype(BF16)
        sib_copy(k).start()
        own[k] = jnp.where(core == 0, low, high)

    def gather_in(k):
        sib_copy(k).wait_recv()
        pair = own[k] + sib_in[k].astype(F32)

        @pl.when(has_outer)
        def _():
            outer_copy(k).wait_recv()
            mine[k] = (pair + outer_in[k].astype(F32)).astype(BF16)

        @pl.when(jnp.logical_not(has_outer))
        def _():
            mine[k] = pair.astype(BF16)

        @pl.when(centre)
        def _():
            cross_copy(k).start()

        @pl.when(jnp.logical_not(centre))
        def _():
            outer_copy(k).start()

    lane = lax.broadcasted_iota(jnp.int32, scales.shape, 1)

    def finish(k, which, summed):
        summed = summed.astype(F32)
        scale = jnp.max(jnp.abs(summed), axis=1, keepdims=True) + 1e-06
        payload = (summed * (1.0 / scale)).astype(BF16)
        fin[k, :, pl.ds(pl.multiple_of(which * BLOCK, BLOCK), BLOCK)] = payload
        scales[...] = jnp.where(lane == k * CORES + which, scale, scales[...])

    def spread(k):
        @pl.when(centre)
        def _():
            cross_copy(k).wait_recv()
            total[k] = (mine[k].astype(F32) + cross_in[k].astype(F32)).astype(BF16)

        @pl.when(jnp.logical_not(centre))
        def _():
            total_copy(k).wait_recv()

        @pl.when(has_outer)
        def _():
            total_copy(k).start()

        share_copy(k).start()
        finish(k, core, total[k])

    def close(k):
        share_copy(k).wait_recv()
        finish(k, 1 - core, sib_total[k])
        out_copy(k).start()

    skew = MID_SKEW + HOP_SKEW * (half - 1 - edge)

    @pl.loop(0, steps + 2 + skew)
    def _(step):
        @pl.when(step < steps)
        def _():
            project(step)

        @pl.when(jnp.logical_and(step >= 1, step < steps + 1))
        def _():
            gather_in(step - 1)

        @pl.when(jnp.logical_and(step >= 1 + skew, step < steps + 1 + skew))
        def _():
            spread(step - 1 - skew)

        @pl.when(step >= 2 + skew)
        def _():
            close(step - 2 - skew)

    scale_copy = pltpu.make_async_copy(scales, scale_hbm, load_sem.at[0])
    scale_copy.start()

    @pl.loop(0, n_ctx - 1 - ctx)
    def _(step):
        for copy in kv_copies(ctx, n_ctx - 1 - step):
            copy.wait_send()

    @pl.loop(0, steps)
    def _(k):
        sib_copy(k).wait_send()
        outer_copy(k).wait_send()
        share_copy(k).wait_send()
        out_copy(k).wait()

        @pl.when(has_outer)
        def _():
            total_copy(k).wait_send()

    scale_copy.wait()


def local(n_ctx, n_tp, queries, keys, values, out_weight, signs):
    rows, depth = queries.shape
    width = out_weight.shape[1]
    heads = depth // HEAD
    kv_group = heads * n_tp // (keys.shape[1] // HEAD)
    steps = width // CHUNK
    blocks = width // BLOCK
    piece = pltpu.VMEM((steps, rows, BLOCK), BF16)
    per_step = pltpu.SemaphoreType.DMA((steps,))
    any_spec = pl.BlockSpec(memory_space=pl.ANY)
    flops = 2 * rows * width * (depth + 2 * CHUNK) + 4 * rows * rows * n_ctx * depth
    return pl.pallas_call(
        functools.partial(kernel, n_ctx, n_tp, kv_group),
        out_shape=(
            jax.ShapeDtypeStruct((rows, width), BF16),
            jax.ShapeDtypeStruct((rows, blocks), F32),
        ),
        in_specs=[any_spec] * 5,
        out_specs=(any_spec, any_spec),
        scratch_shapes=[
            pltpu.VMEM((rows, depth), BF16),
            pltpu.VMEM((blocks, BLOCK), jnp.int32),
            pltpu.VMEM((n_ctx, rows, HEAD), BF16),
            pltpu.VMEM((n_ctx, rows, HEAD), BF16),
            pltpu.VMEM((steps, depth, CHUNK), BF16),
            pltpu.VMEM((rows, depth), BF16),
            pltpu.VMEM((heads, 1, rows), F32),
            pltpu.VMEM((heads, 1, rows), F32),
            pltpu.VMEM((heads, HEAD, rows), F32),
            pltpu.VMEM((CHUNK, CHUNK), BF16),
            pltpu.VMEM((CHUNK, CHUNK), BF16),
            pltpu.VMEM((steps, rows, BLOCK), F32),
            piece,
            piece,
            piece,
            piece,
            piece,
            piece,
            piece,
            pltpu.VMEM((steps, rows, CHUNK), BF16),
            pltpu.VMEM((rows, blocks), F32),
            pltpu.SemaphoreType.DMA((4,)),
            per_step,
            pltpu.SemaphoreType.DMA((2, n_ctx)),
            pltpu.SemaphoreType.DMA((2, n_ctx)),
            per_step,
            per_step,
            per_step,
            per_step,
            per_step,
            per_step,
            per_step,
            per_step,
            per_step,
            per_step,
        ],
        compiler_params=pltpu.CompilerParams(
            collective_id=0, has_side_effects=True, vmem_limit_bytes=54 * 1024 * 1024
        ),
        cost_estimate=pl.CostEstimate(
            flops=flops, bytes_accessed=2 * depth * width + 4 * rows * width, transcendentals=0
        ),
    )(queries, keys, values, out_weight, signs.reshape(blocks, BLOCK))


def solution(mesh):
    n_ctx, n_tp = mesh.shape["ctx"], mesh.shape["tp"]
    return jax.shard_map(
        functools.partial(local, n_ctx, n_tp),
        mesh=mesh,
        in_specs=(P("ctx", "tp"), P("ctx", None), P("ctx", None), P("tp", None), P()),
        out_specs=(P("ctx", None), P("ctx", None)),
        check_vma=False,
    )
```
